32 devices in a mesh: group: 2 (over y), tenant: 4 (over x, core), mp: 4 (over z).
Axes of the slice: x: 2, y: 2, z: 4, core: 2. Of those that a mesh axis runs over, the one named last changes fastest.
Arguments:
- tokens: bfloat16 [8192, 8192], P(('group', 'tenant'), 'mp'), parts along dimension 0, may hold values from -6 to 6
- kv_weight: bfloat16 [8192, 2, 1024], P(None, None, 'mp'), may hold values from -0.0625 to 0.0625
- delta_in: bfloat16 [48, 64, 8192], P(('group', 'tenant'), None, 'mp'), parts along dimension 0, may hold values from -0.0625 to 0.0625
- delta_out: bfloat16 [48, 64, 2, 1024], P(('group', 'tenant'), None, None, 'mp'), parts along dimension 0, may hold values from -0.75 to 0.75
- delta_scale: bfloat16 [48, 64], P(('group', 'tenant')), parts along dimension 0, may hold values from 0.29882812 to 3
- owner_map: int32 [48], P('group'), parts along dimension 0, may hold values from 0 to 23, as said below
- resp_tenant: int32 [16], P(('group', 'tenant')), parts along dimension 0, may hold values from 0 to 23, as said below
Outputs:
- keys_values: bfloat16 [8192, 2, 1024], P(('group', 'tenant'), None, 'mp'), parts along dimension 0
The draws below stay inside these ranges and needn't reach their ends.
There are 2 independent parts, one for each index of `group`. The reference program is written for one: setup_inputs(seed, part) draws one part's arguments, and reference() takes and returns one part's arrays. A program takes and returns all parts, laid end to end along the dimension named above; an argument that names none is the same for every part. Nothing has to cross between parts.
Inputs may be any that keep to these rules, and one draw needn't show every extreme that they name: A permutation: tenant t's factors are in store row owner_map[t], which lies with owner owner_map[t] // 6. `resp_tenant`: exactly 4 distinct tenants are named over all responses; their store rows fall on at most 2 distinct rows of any one owner: a quarter of the owners hold 2 named tenants, a quarter none, the others one.
All inputs are finite; a program needn't handle non-finite values.
Results may differ from the reference program's by a relative error of at most 0.0044.
Values may be sent and summed in bfloat16 or wider, within the bound.
No kernel may reach another device: no remote copies, remote signals or barrier semaphores. Data moves between devices by JAX's collectives and lax.ppermute only.
A program may use at most 128 MiB of HBM per device.

```python
import math
import jax
import jax.numpy as jnp
from jax import lax

D = 8192
R = 64
LEN = 512
TEN_DEV = 6
KVW = 1024
RESPONSES = 8
TOKENS = 4096
TENANTS = 24
N_TENANT = 4


def request_plan(key):
    keys = jax.random.split(key, 7)
    owner_map = jax.random.permutation(keys[0], TENANTS).astype(jnp.int32)
    owner_rank = jnp.argsort(jax.random.permutation(keys[1], N_TENANT))
    counts = jnp.where(owner_rank < N_TENANT // 4, 2, jnp.where(owner_rank < N_TENANT // 2, 0, 1))
    offsets = jax.random.randint(keys[2], (N_TENANT,), 0, TEN_DEV)
    owners = jnp.arange(N_TENANT, dtype=jnp.int32)
    first = owners * TEN_DEV + offsets
    second = owners * TEN_DEV + (offsets + 1) % TEN_DEV
    candidates = jnp.stack([first, second], axis=1).reshape(-1)
    usable = jnp.stack([counts >= 1, counts >= 2], axis=1).reshape(-1)
    ranking = jnp.argsort(1 - usable.astype(jnp.int32), stable=True)
    named = candidates[ranking][:N_TENANT]
    named = named[jax.random.permutation(keys[3], N_TENANT)]
    extra_count = RESPONSES - N_TENANT
    skewed = jnp.minimum(jax.random.randint(keys[4], (extra_count,), 0, N_TENANT), jax.random.randint(keys[5], (extra_count,), 0, N_TENANT))
    picks = jnp.concatenate([jnp.arange(N_TENANT, dtype=jnp.int32), skewed.astype(jnp.int32)])
    picks = picks[jax.random.permutation(keys[6], RESPONSES)]
    inverse = jnp.argsort(owner_map)
    return (owner_map, inverse[named[picks]].astype(jnp.int32))


def draw_owner_map(key, part):
    return request_plan(key)[0]


def draw_resp_tenant(key, part):
    return request_plan(key)[1]


def levels(stream_key, shape, pieces, least, largest):
    def one(axis_at, parts):
        heights = jax.random.uniform(jax.random.fold_in(jax.random.fold_in(stream_key, 6), axis_at), (parts,), jnp.float32, least / len(pieces), largest / len(pieces))
        return jnp.repeat(jnp.exp(heights), shape[axis_at] // parts).reshape((-1,) + (1,) * (len(shape) - axis_at - 1))

    factor_of = one(*pieces[0])
    for cut in pieces[1:]:
        factor_of = factor_of * one(*cut)
    return factor_of


def bell_draw(key, extent, spread, reach, pieces=(), held_as=jnp.bfloat16):
    entries = spread * jax.random.normal(key, extent, jnp.float32)
    if pieces:
        entries = entries * levels(key, extent, pieces, -0.22, 0.18)
    return jnp.clip(entries, -reach, reach).astype(held_as)


def setup_inputs(seed: int = 0, part: int = 0) -> dict:
    seeds = jax.random.split(jax.random.key(seed), 8)
    part_splits = jax.random.split(jax.random.fold_in(seeds[7], part), 8)
    tokens = bell_draw(part_splits[0], (TOKENS, D), 1.0, 6.0, ((0, 4), (1, 4)))
    kv_weight = bell_draw(seeds[1], (D, 2, KVW), D ** -0.5, 0.0625, ((2, 4),))
    delta_in = bell_draw(part_splits[2], (TENANTS, R, D), D ** -0.5, 0.0625, ((0, 4), (2, 4)))
    delta_out = bell_draw(part_splits[3], (TENANTS, R, 2, KVW), R ** -0.5, 0.75, ((0, 4), (3, 4)))
    delta_scale = jnp.clip(jnp.exp(math.log(3.0) - 2.306499 * jax.random.uniform(part_splits[4], (TENANTS, R), jnp.float32) ** levels(part_splits[4], (TENANTS, R), ((0, 4),), -0.2, 0.2)), 0.29882812, 3.0).astype(jnp.bfloat16)
    owner_map = draw_owner_map(jax.random.fold_in(jax.random.fold_in(seeds[7], part), 71), part)
    resp_tenant = draw_resp_tenant(jax.random.fold_in(jax.random.fold_in(seeds[7], part), 71), part)
    return {"tokens": tokens, "kv_weight": kv_weight, "delta_in": delta_in, "delta_out": delta_out, "delta_scale": delta_scale, "owner_map": owner_map, "resp_tenant": resp_tenant}


def reference(tokens, kv_weight, delta_in, delta_out, delta_scale, owner_map, resp_tenant):
    slots = jnp.take(owner_map, resp_tenant).astype(jnp.int32)
    flat_weight = kv_weight.reshape(D, 2 * KVW)
    base = jnp.dot(tokens, flat_weight, preferred_element_type=jnp.float32)

    def one_response(inputs):
        rows, slot_id = inputs
        factor_in = delta_in[slot_id]
        coeff = jnp.dot(rows, factor_in.T, preferred_element_type=jnp.float32)
        lowrank = (coeff * delta_scale[slot_id].astype(jnp.float32)[None, :]).astype(jnp.bfloat16)
        factor_out = delta_out[slot_id].reshape(R, 2 * KVW)
        return jnp.dot(lowrank, factor_out, preferred_element_type=jnp.float32)

    delta = lax.map(one_response, (tokens.reshape(RESPONSES, LEN, D), slots))
    total = base + delta.reshape(TOKENS, 2 * KVW)
    return total.astype(jnp.bfloat16).reshape(TOKENS, 2, KVW)
```

```python
import jax
import jax.numpy as jnp
from jax import lax
from jax.sharding import PartitionSpec as P

CAPO = 2
F32 = jnp.float32
BF16 = jnp.bfloat16


def swap(value, axis, size, mask):
    return lax.ppermute(value, axis, [(i, i ^ mask) for i in range(size)])


def hop(value, n, at):
    return lax.ppermute(value, "mp", [(at, at + 1), (n - 1 - at, n - 2 - at)])


def shards(tokens, kv_weight, delta_in, delta_out, delta_scale, owner_map, resp_tenant):
    tok_dev, d_shard = tokens.shape
    resp_dev = resp_tenant.shape[0]
    resp_len = tok_dev // resp_dev
    ten_dev, rank = delta_in.shape[0], delta_in.shape[1]
    head_cols = kv_weight.shape[2]
    cols = 2 * head_cols
    n_group = lax.axis_size("group")
    n_owner = lax.axis_size("tenant")
    n = lax.axis_size("mp")
    plane = n_group * n_owner
    share_rows = d_shard // plane
    tenants = owner_map.shape[0]
    me_mp = lax.axis_index("mp")
    me_owner = lax.axis_index("tenant")
    me_share = lax.axis_index("group") * n_owner + me_owner
    hop_type = BF16 if n <= 4 else F32

    def weight_pieces(k):
        row = (me_mp ^ k) * d_shard + me_share * share_rows
        part = lax.dynamic_slice_in_dim(kv_weight, row, share_rows, 0).reshape(share_rows, cols)
        arrived = swap(part, "mp", n, k)
        pieces = [arrived] + [
            swap(arrived, ("group", "tenant"), plane, mask) for mask in range(2, plane, 2)
        ]
        mine = jnp.concatenate(pieces, axis=0)
        other = swap(mine, "tenant", n_owner, 1)
        return mine, other

    blocks_of = tokens.reshape(tok_dev, plane, share_rows)
    order = [m for m in range(0, plane, 2)] + [m ^ 1 for m in range(0, plane, 2)]
    ordered = jnp.concatenate(
        [lax.dynamic_index_in_dim(blocks_of, me_share ^ m, 1, keepdims=False) for m in order], axis=1
    )

    def partial_of(k):
        mine, other = weight_pieces(k)
        return jnp.dot(ordered, jnp.concatenate([mine, other], axis=0), preferred_element_type=F32)

    tenant_ids = jnp.arange(tenants, dtype=jnp.int32)
    my_slot = jnp.sum(
        jnp.where(resp_tenant[:, None] == tenant_ids[None, :], owner_map[None, :], 0), axis=1
    )
    requests = jnp.concatenate(
        [my_slot] + [swap(my_slot, "tenant", n_owner, m) for m in range(1, n_owner)]
    )
    stored = me_owner * ten_dev + jnp.arange(ten_dev, dtype=jnp.int32)
    wanted = jnp.any(requests[None, :] == stored[:, None], axis=1)
    ranking = jnp.cumsum(wanted.astype(jnp.int32)) - 1
    rows, names = [], []
    for c in range(CAPO):
        hit = wanted & (ranking == c)
        at = jnp.sum(jnp.where(hit, jnp.arange(ten_dev, dtype=jnp.int32), 0))
        rows.append(at)
        names.append(jnp.where(jnp.any(hit), me_owner * ten_dev + at, -1))
    name = jnp.stack(names)

    def pack(store):
        return jnp.stack([lax.dynamic_index_in_dim(store, at, 0, keepdims=False) for at in rows])

    def spread(packed):
        mine = jnp.concatenate(
            [packed] + [swap(packed, "tenant", n_owner, m) for m in range(2, n_owner, 2)], axis=0
        )
        return jnp.concatenate([mine, swap(mine, "tenant", n_owner, 1)], axis=0)

    all_names = spread(name)
    all_in = spread(pack(delta_in))
    all_out = spread(pack(delta_out).reshape(CAPO, rank, cols))
    all_scale = spread(pack(delta_scale))
    picked = [jnp.argmax(all_names == my_slot[r]).astype(jnp.int32) for r in range(resp_dev)]

    def choose(store):
        return jnp.stack([lax.dynamic_index_in_dim(store, at, 0, keepdims=False) for at in picked])

    part_coeff = jnp.einsum(
        "rld,rkd->rlk",
        tokens.reshape(resp_dev, resp_len, d_shard),
        choose(all_in),
        preferred_element_type=F32,
    )
    coeff, came = part_coeff, None
    for h in range(n - 1):
        came = hop(part_coeff if came is None else part_coeff + came, n, h)
        coeff = coeff + came
    lowrank = (coeff * choose(all_scale).astype(F32)[:, None, :]).astype(BF16)
    delta = jnp.einsum(
        "rlk,rkc->rlc", lowrank, choose(all_out), preferred_element_type=F32
    ).reshape(tok_dev, cols)

    own = lax.dynamic_slice_in_dim(kv_weight, me_mp * d_shard, d_shard, 0).reshape(d_shard, cols)
    parts = {k: partial_of(k) for k in range(n - 1, 0, -1)}
    came = []
    for s in range(1, n):
        now = []
        for h in range(s):
            load = parts[h ^ (h + n - s)]
            if h:
                load = load + came[h - 1].astype(F32)
            now.append(hop(load.astype(hop_type), n, h))
        came = now
    total = jnp.dot(tokens, own, preferred_element_type=F32) + delta
    for value in came:
        total = total + value.astype(F32)
    return total.astype(BF16).reshape(tok_dev, 2, head_cols)


def solution(mesh):
    return jax.shard_map(
        shards,
        mesh=mesh,
        in_specs=(
            P(("group", "tenant"), "mp"),
            P(None, None, "mp"),
            P(("group", "tenant"), None, "mp"),
            P(("group", "tenant"), None, None, "mp"),
            P(("group", "tenant"), None),
            P("group"),
            P(("group", "tenant")),
        ),
        out_specs=P(("group", "tenant"), None, "mp"),
        check_vma=False,
    )
```

```python
import functools

import jax
import jax.numpy as jnp
from jax import lax
from jax.experimental import pallas as pl
from jax.experimental.pallas import tpu as pltpu
from jax.sharding import PartitionSpec as P

CAPO = 2
F32 = jnp.float32
BF16 = jnp.bfloat16
I32 = jnp.int32
VMEM_LIMIT = 60 * 1024 * 1024
SMALL = pl.CostEstimate(flops=1, bytes_accessed=1, transcendentals=0)


def swap(value, axis, size, mask):
    return lax.ppermute(value, axis, [(i, i ^ mask) for i in range(size)])


def hop(value, n, at):
    return lax.ppermute(value, "mp", [(at, at + 1), (n - 1 - at, n - 2 - at)])


def tied(value, *others):
    return lax.optimization_barrier((value, *others))[0]


def partial_kernel(masks, share_ref, tok_ref, *refs):
    pieces = refs[: len(masks)]
    low_ref, full_ref, weight = refs[len(masks) :]
    rows = weight.shape[0] // len(masks)

    @pl.when(pl.program_id(0) == 0)
    def _():
        for mask, piece in zip(masks, pieces):
            to = pl.multiple_of((share_ref[0] ^ mask) * rows, rows)
            weight[pl.ds(to, rows), :] = piece[...]

    product = jnp.dot(tok_ref[...], weight[...], preferred_element_type=F32)
    full_ref[...] = product
    low_ref[...] = product.astype(low_ref.dtype)


def partial_product(share, tokens, pieces, low_type):
    tok_dev, depth = tokens.shape
    masks, pieces = tuple(pieces), tuple(pieces.values())
    cols = pieces[0].shape[1]
    tile = min(256, tok_dev)
    whole = lambda i, s: (0, 0)
    row = lambda i, s: (i, 0)
    return pl.pallas_call(
        functools.partial(partial_kernel, masks),
        out_shape=(
            jax.ShapeDtypeStruct((tok_dev, cols), low_type),
            jax.ShapeDtypeStruct((tok_dev, cols), F32),
        ),
        grid_spec=pltpu.PrefetchScalarGridSpec(
            num_scalar_prefetch=1,
            grid=(tok_dev // tile,),
            in_specs=[pl.BlockSpec((tile, depth), row)]
            + [pl.BlockSpec(piece.shape, whole) for piece in pieces],
            out_specs=(pl.BlockSpec((tile, cols), row), pl.BlockSpec((tile, cols), row)),
            scratch_shapes=[pltpu.VMEM((depth, cols), BF16)],
        ),
        compiler_params=pltpu.CompilerParams(vmem_limit_bytes=VMEM_LIMIT),
        cost_estimate=SMALL,
        name="partial_product",
    )(share, tokens, *pieces)


def pack_kernel(n_owner, ten_dev, resp_dev, owner_ref, map_ref, *refs):
    asked_refs = refs[:n_owner]
    in_ref, out_ref, in_to, out_to, pick_ref, sems = refs[n_owner:]
    me = owner_ref[0]
    asked = [map_ref[ref[r]] for ref in asked_refs for r in range(resp_dev)]

    def is_asked(slot):
        hits = [slot == other for other in asked]
        return functools.reduce(jnp.logical_or, hits).astype(I32)

    found = I32(0)
    first, second = I32(0), I32(0)
    for j in range(ten_dev):
        hit = is_asked(me * ten_dev + j)
        first = jnp.where((hit == 1) & (found == 0), j, first)
        second = jnp.where((hit == 1) & (found == 1), j, second)
        found = found + hit
    copies = []
    for c, at in enumerate((first, second)):
        copies.append(pltpu.make_async_copy(in_ref.at[at], in_to.at[c], sems.at[2 * c]))
        copies.append(pltpu.make_async_copy(out_ref.at[at], out_to.at[c], sems.at[2 * c + 1]))
    for copy in copies:
        copy.start()
    for r in range(resp_dev):
        slot = asked[r]
        owner = lax.div(slot, I32(ten_dev))
        before = I32(0)
        for j in range(ten_dev):
            other = owner * ten_dev + j
            before = before + jnp.where(other < slot, is_asked(other), 0)
        mask = owner ^ me
        pick_ref[r] = ((mask >> 1) + (mask & 1) * (n_owner // 2)) * CAPO + before
    for copy in copies:
        copy.wait()


def pack(owner, owner_map, asked, delta_in, out_rows):
    ten_dev = delta_in.shape[0]
    smem = pl.BlockSpec(memory_space=pltpu.SMEM)
    hbm = pl.BlockSpec(memory_space=pl.ANY)
    vmem = pl.BlockSpec(memory_space=pltpu.VMEM)
    return pl.pallas_call(
        functools.partial(pack_kernel, len(asked), ten_dev, asked[0].shape[0]),
        out_shape=(
            jax.ShapeDtypeStruct((CAPO,) + delta_in.shape[1:], BF16),
            jax.ShapeDtypeStruct((CAPO,) + out_rows.shape[1:], BF16),
            jax.ShapeDtypeStruct(asked[0].shape, I32),
        ),
        in_specs=[smem] * (2 + len(asked)) + [hbm, hbm],
        out_specs=(vmem, vmem, smem),
        scratch_shapes=[pltpu.SemaphoreType.DMA((2 * CAPO,))],
        compiler_params=pltpu.CompilerParams(vmem_limit_bytes=VMEM_LIMIT),
        cost_estimate=SMALL,
        name="pack_named",
    )(owner, owner_map, *asked, delta_in, out_rows)


def coeff_kernel(pick_ref, tok_ref, mine_ref, other_ref, coeff_ref, *, half):
    here = pick_ref[pl.program_id(0)] < half
    factor = jnp.where(here, mine_ref[...].astype(F32), other_ref[...].astype(F32)).astype(BF16)
    coeff_ref[...] = lax.dot_general(
        factor, tok_ref[...], (((1,), (1,)), ((), ())), preferred_element_type=F32
    )


def coefficients(pick, tokens, mine, other, resp_len):
    depth = tokens.shape[1]
    half, rank = mine.shape[0], mine.shape[1]
    resp_dev = pick.shape[0]
    return pl.pallas_call(
        functools.partial(coeff_kernel, half=half),
        out_shape=jax.ShapeDtypeStruct((resp_dev, rank, resp_len), F32),
        grid_spec=pltpu.PrefetchScalarGridSpec(
            num_scalar_prefetch=1,
            grid=(resp_dev,),
            in_specs=[
                pl.BlockSpec((resp_len, depth), lambda r, p: (r, 0)),
                pl.BlockSpec((None, rank, depth), lambda r, p: (jnp.minimum(p[r], half - 1), 0, 0)),
                pl.BlockSpec((None, rank, depth), lambda r, p: (jnp.maximum(p[r] - half, 0), 0, 0)),
            ],
            out_specs=pl.BlockSpec((None, rank, resp_len), lambda r, p: (r, 0, 0)),
        ),
        compiler_params=pltpu.CompilerParams(vmem_limit_bytes=VMEM_LIMIT),
        cost_estimate=SMALL,
        name="coefficients",
    )(pick, tokens, mine, other)


def shards(tokens, kv_weight, delta_in, delta_out, delta_scale, owner_map, resp_tenant):
    tok_dev, d_shard = tokens.shape
    resp_dev = resp_tenant.shape[0]
    resp_len = tok_dev // resp_dev
    rank = delta_in.shape[1]
    head_cols = kv_weight.shape[2]
    cols = 2 * head_cols
    n_owner = lax.axis_size("tenant")
    n = lax.axis_size("mp")
    plane = lax.axis_size("group") * n_owner
    share_rows = d_shard // plane
    me_mp = lax.axis_index("mp")
    me_owner = lax.axis_index("tenant")
    me_share = lax.axis_index("group") * n_owner + me_owner
    share = me_share.astype(I32).reshape(1)
    hop_type = BF16 if n <= 4 else F32

    def sent(k):
        row = (me_mp ^ k) * d_shard + me_share * share_rows
        return lax.dynamic_slice_in_dim(kv_weight, row, share_rows, 0).reshape(share_rows, cols)

    def shared(arrived):
        pieces = {0: arrived}
        for mask in range(2, plane, 2):
            pieces[mask] = swap(arrived, ("group", "tenant"), plane, mask)
        for mask in range(0, plane, 2):
            pieces[mask | 1] = swap(pieces[mask], "tenant", n_owner, 1)
        return pieces

    order = list(range(n - 1, 0, -1))
    low, full, before = {}, {}, []
    last = None
    for k in order:
        block = sent(k) if last is None else tied(sent(k), last)
        last = swap(block, "mp", n, k)
        here = tied(last, low[k + 1]) if k + 1 in low else last
        pieces = shared(here)
        before.append(pieces[plane - 2])
        low[k], full[k] = partial_product(share, tokens, pieces, hop_type)

    asked = [resp_tenant] + [swap(resp_tenant, "tenant", n_owner, m) for m in range(1, n_owner)]
    pad = ((0, 0), (0, 0), (0, 1), (0, head_cols - rank))
    out_rows = jnp.concatenate([delta_out, jnp.pad(delta_scale[:, None, None, :], pad)], axis=1)
    packed_in, packed_out, pick = pack(
        me_owner.astype(I32).reshape(1), owner_map, asked, delta_in, out_rows
    )

    def spread(packed):
        mine = jnp.concatenate(
            [packed] + [swap(packed, "tenant", n_owner, m) for m in range(2, n_owner, 2)], axis=0
        )
        return mine, swap(mine, "tenant", n_owner, 1)

    packed_in = tied(packed_in, before[0])
    part_coeff = coefficients(pick, tokens, *spread(packed_in), resp_len)
    coeff, came = part_coeff, None
    for h in range(n - 1):
        came = hop(part_coeff if came is None else part_coeff + came, n, h)
        coeff = coeff + came
    all_out = jnp.concatenate(spread(packed_out), axis=0)
    chosen = jnp.stack(
        [lax.dynamic_index_in_dim(all_out, pick[r], 0, keepdims=False) for r in range(resp_dev)]
    )
    scale = chosen[:, rank, 0, :rank].astype(F32)
    lowrank = (coeff * scale[:, :, None]).astype(BF16)
    delta = jnp.einsum(
        "rkl,rkc->rlc",
        lowrank,
        chosen[:, :rank].reshape(resp_dev, rank, cols),
        preferred_element_type=F32,
    ).reshape(tok_dev, cols)
    own = lax.dynamic_slice_in_dim(kv_weight, me_mp * d_shard, d_shard, 0).reshape(d_shard, cols)
    base = jnp.dot(tokens, own, preferred_element_type=F32) + delta

    came = []
    for s in range(1, n):
        now = []
        for h in range(s):
            k = h ^ (h + n - s)
            load = low[k] if h == 0 else (full[k] + came[h - 1].astype(F32)).astype(hop_type)
            now.append(hop(load, n, h))
        came = now
    total = lax.optimization_barrier(base)
    for value in came:
        total = total + value.astype(F32)
    return total.astype(BF16).reshape(tok_dev, 2, head_cols)


def solution(mesh):
    return jax.shard_map(
        shards,
        mesh=mesh,
        in_specs=(
            P(("group", "tenant"), "mp"),
            P(None, None, "mp"),
            P(("group", "tenant"), None, "mp"),
            P(("group", "tenant"), None, None, "mp"),
            P(("group", "tenant"), None),
            P("group"),
            P(("group", "tenant")),
        ),
        out_specs=P(("group", "tenant"), None, "mp"),
        check_vma=False,
    )
```

```python
import functools

import jax
import jax.numpy as jnp
from jax import lax
from jax.experimental import pallas as pl
from jax.experimental.pallas import tpu as pltpu
from jax.sharding import PartitionSpec as P

CAPO = 2
F32 = jnp.float32
BF16 = jnp.bfloat16
I32 = jnp.int32
VMEM_LIMIT = 60 * 1024 * 1024
SMALL = pl.CostEstimate(flops=1, bytes_accessed=1, transcendentals=0)
LARGE = pl.CostEstimate(flops=20_000_000_000, bytes_accessed=1, transcendentals=0)


def swap(value, axis, size, mask):
    return lax.ppermute(value, axis, [(i, i ^ mask) for i in range(size)])


def hop(value, n, at):
    return lax.ppermute(value, "mp", [(at, at + 1), (n - 1 - at, n - 2 - at)])


def stages(n):
    if n == 4:
        return [(3, 0, 3, 0), (2, 3, 0, 1), (1, 2, 1, 2)]
    return [tuple(m ^ k for m in range(n)) for k in range(n - 1, 0, -1)]


def rounds(targets):
    left, out = [(source, m) for m, source in enumerate(targets)], []
    while left:
        now, rest = {}, []
        for source, m in left:
            if source in now or (len(targets) == 4 and (source ^ m) != (left[0][0] ^ left[0][1])):
                rest.append((source, m))
            else:
                now[source] = m
        out.append(list(now.items()))
        left = rest
    return out


def tied(value, *others):
    return lax.optimization_barrier((value, *others))[0]


def gate(values, *others):
    kept = lax.optimization_barrier((*values.values(), *others))
    return dict(zip(values, kept))


def step_kernel(masks, arrivals, earlier, place_ref, tok_ref, *refs):
    count = len(masks)
    pieces, refs = refs[:count], refs[count:]
    extra, refs = refs[: arrivals + earlier], refs[arrivals + earlier :]
    *out_refs, weight, token, total, held, sems, held_sems = refs
    rows = weight.shape[1]
    copies = []
    for at, mask in enumerate(masks):
        here = pl.ds(pl.multiple_of((place_ref[0] ^ mask) * rows, rows), rows)
        copies.append(
            (
                pltpu.make_async_copy(pieces[at], weight.at[at], sems.at[0, at]),
                pltpu.make_async_copy(tok_ref.at[:, here], token.at[at], sems.at[1, at]),
            )
        )
    late = [
        pltpu.make_async_copy(ref, held.at[at], held_sems.at[at]) for at, ref in enumerate(extra)
    ]
    for pair in copies:
        for copy in pair:
            copy.start()
    for copy in late:
        copy.start()
    for at, pair in enumerate(copies):
        for copy in pair:
            copy.wait()
        product = jnp.dot(token[at], weight[at], preferred_element_type=F32)
        if at:
            product = total[...] + product
        if at < count - 1 or late:
            total[...] = product
        else:
            out_refs[0][...] = product.astype(out_refs[0].dtype)
    for copy in late:
        copy.wait()
    if late:
        finish(arrivals, earlier, place_ref, total, held, out_refs)


def finish(arrivals, earlier, place_ref, total, held, out_refs):
    for at, ref in enumerate(out_refs):

        def put(mine, ref=ref, at=at):
            ref[...] = (mine[...].astype(F32) + held[at].astype(F32)).astype(ref.dtype)

        if earlier:
            pl.when(place_ref[1 + at] == 1)(lambda put=put: put(held.at[arrivals]))
            pl.when(place_ref[1 + at] != 1)(lambda put=put: put(total))
        else:
            put(total)


def thin_kernel(masks, arrivals, earlier, place_ref, tok_ref, *refs):
    pieces, refs = refs[: len(masks)], refs[len(masks) :]
    extra, refs = refs[: arrivals + earlier], refs[arrivals + earlier :]
    *out_refs, weight, total, held, held_sems = refs
    rows = pieces[0].shape[0]
    late = [
        pltpu.make_async_copy(ref, held.at[at], held_sems.at[at]) for at, ref in enumerate(extra)
    ]
    for copy in late:
        copy.start()
    for mask, piece in zip(masks, pieces):
        to = pl.multiple_of((place_ref[0] ^ mask) * rows, rows)
        weight[pl.ds(to, rows), :] = piece[...]
    total[...] = jnp.dot(tok_ref[...], weight[...], preferred_element_type=F32)
    for copy in late:
        copy.wait()
    if late:
        finish(arrivals, earlier, place_ref, total, held, out_refs)
    else:
        out_refs[0][...] = total[...].astype(out_refs[0].dtype)


def step(place, tokens, pieces, arrivals, earlier, outs, out_type, cost):
    tok_dev, depth = tokens.shape
    masks, pieces = tuple(pieces), tuple(pieces.values())
    rows, cols = pieces[0].shape
    count = len(pieces)
    extra = len(arrivals) + len(earlier)
    vmem = pl.BlockSpec(memory_space=pltpu.VMEM)
    far = pl.BlockSpec(memory_space=pl.ANY)
    held = [pltpu.VMEM((max(extra, 1), tok_dev, cols), out_type)]
    total = [pltpu.VMEM((tok_dev, cols), F32)]
    held_sems = [pltpu.SemaphoreType.DMA((max(extra, 1),))]
    if rows % 128:
        kernel, where = thin_kernel, vmem
        scratch = [pltpu.VMEM((depth, cols), BF16)] + total + held + held_sems
    else:
        kernel, where = step_kernel, far
        scratch = [
            pltpu.VMEM((count, rows, cols), BF16),
            pltpu.VMEM((count, tok_dev, rows), BF16),
        ]
        scratch += total + held + [pltpu.SemaphoreType.DMA((2, count))] + held_sems
    return pl.pallas_call(
        functools.partial(kernel, masks, len(arrivals), len(earlier)),
        out_shape=[jax.ShapeDtypeStruct((tok_dev, cols), out_type)] * outs,
        in_specs=[pl.BlockSpec(memory_space=pltpu.SMEM)] + [where] * (1 + count) + [far] * extra,
        out_specs=[vmem] * outs,
        scratch_shapes=scratch,
        compiler_params=pltpu.CompilerParams(vmem_limit_bytes=VMEM_LIMIT),
        cost_estimate=cost,
        name="walk_step",
    )(place, tokens, *pieces, *arrivals, *earlier)


def pack_kernel(n_owner, ten_dev, resp_dev, owner_ref, map_ref, *refs):
    asked_refs = refs[:n_owner]
    in_ref, out_ref, in_to, out_to, pick_ref, sems = refs[n_owner:]
    me = owner_ref[0]
    asked = [map_ref[ref[r]] for ref in asked_refs for r in range(resp_dev)]

    def is_asked(slot):
        hits = [slot == other for other in asked]
        return functools.reduce(jnp.logical_or, hits).astype(I32)

    found = I32(0)
    first, second = I32(0), I32(0)
    for j in range(ten_dev):
        hit = is_asked(me * ten_dev + j)
        first = jnp.where((hit == 1) & (found == 0), j, first)
        second = jnp.where((hit == 1) & (found == 1), j, second)
        found = found + hit
    copies = []
    for c, at in enumerate((first, second)):
        copies.append(pltpu.make_async_copy(in_ref.at[at], in_to.at[c], sems.at[2 * c]))
        copies.append(pltpu.make_async_copy(out_ref.at[at], out_to.at[c], sems.at[2 * c + 1]))
    for copy in copies:
        copy.start()
    for r in range(resp_dev):
        slot = asked[r]
        owner = lax.div(slot, I32(ten_dev))
        before = I32(0)
        for j in range(ten_dev):
            other = owner * ten_dev + j
            before = before + jnp.where(other < slot, is_asked(other), 0)
        mask = owner ^ me
        pick_ref[r] = ((mask >> 1) + (mask & 1) * (n_owner // 2)) * CAPO + before
    for copy in copies:
        copy.wait()


def pack(owner, owner_map, asked, delta_in, out_rows):
    ten_dev = delta_in.shape[0]
    smem = pl.BlockSpec(memory_space=pltpu.SMEM)
    hbm = pl.BlockSpec(memory_space=pl.ANY)
    vmem = pl.BlockSpec(memory_space=pltpu.VMEM)
    return pl.pallas_call(
        functools.partial(pack_kernel, len(asked), ten_dev, asked[0].shape[0]),
        out_shape=(
            jax.ShapeDtypeStruct((CAPO,) + delta_in.shape[1:], BF16),
            jax.ShapeDtypeStruct((CAPO,) + out_rows.shape[1:], BF16),
            jax.ShapeDtypeStruct(asked[0].shape, I32),
        ),
        in_specs=[smem] * (2 + len(asked)) + [hbm, hbm],
        out_specs=(vmem, vmem, smem),
        scratch_shapes=[pltpu.SemaphoreType.DMA((2 * CAPO,))],
        compiler_params=pltpu.CompilerParams(vmem_limit_bytes=VMEM_LIMIT),
        cost_estimate=LARGE,
        name="pack_named",
    )(owner, owner_map, *asked, delta_in, out_rows)


def coeff_kernel(pick_ref, tok_ref, mine_ref, other_ref, coeff_ref, *, half):
    here = pick_ref[pl.program_id(0)] < half
    factor = jnp.where(here, mine_ref[...].astype(F32), other_ref[...].astype(F32)).astype(BF16)
    coeff_ref[...] = lax.dot_general(
        factor, tok_ref[...], (((1,), (1,)), ((), ())), preferred_element_type=F32
    )


def coefficients(pick, tokens, mine, other, resp_len):
    depth = tokens.shape[1]
    half, rank = mine.shape[0], mine.shape[1]
    resp_dev = pick.shape[0]
    return pl.pallas_call(
        functools.partial(coeff_kernel, half=half),
        out_shape=jax.ShapeDtypeStruct((resp_dev, rank, resp_len), F32),
        grid_spec=pltpu.PrefetchScalarGridSpec(
            num_scalar_prefetch=1,
            grid=(resp_dev,),
            in_specs=[
                pl.BlockSpec((resp_len, depth), lambda r, p: (r, 0)),
                pl.BlockSpec((None, rank, depth), lambda r, p: (jnp.minimum(p[r], half - 1), 0, 0)),
                pl.BlockSpec((None, rank, depth), lambda r, p: (jnp.maximum(p[r] - half, 0), 0, 0)),
            ],
            out_specs=pl.BlockSpec((None, rank, resp_len), lambda r, p: (r, 0, 0)),
        ),
        compiler_params=pltpu.CompilerParams(vmem_limit_bytes=VMEM_LIMIT),
        cost_estimate=SMALL,
        name="coefficients",
    )(pick, tokens, mine, other)


def shards(tokens, kv_weight, delta_in, delta_out, delta_scale, owner_map, resp_tenant):
    tok_dev, d_shard = tokens.shape
    resp_dev = resp_tenant.shape[0]
    resp_len = tok_dev // resp_dev
    rank = delta_in.shape[1]
    head_cols = kv_weight.shape[2]
    cols = 2 * head_cols
    n_owner = lax.axis_size("tenant")
    n = lax.axis_size("mp")
    plane = lax.axis_size("group") * n_owner
    share_rows = d_shard // plane
    me_mp = lax.axis_index("mp")
    me_owner = lax.axis_index("tenant")
    me_share = lax.axis_index("group") * n_owner + me_owner
    share = me_share.astype(I32).reshape(1)
    hop_type = BF16 if n <= 4 else F32

    def part_for(pairs):
        to = sum(jnp.where(me_mp == source, target, 0) for source, target in pairs)
        row = to * d_shard + me_share * share_rows
        return lax.dynamic_slice_in_dim(kv_weight, row, share_rows, 0).reshape(share_rows, cols)

    def arrival(targets, *waits):
        return sum(
            lax.ppermute(tied(part_for(pairs), *waits), "mp", pairs) for pairs in rounds(targets)
        )

    def crossed(arrived):
        pieces = {0: arrived}
        for mask in range(2, plane, 2):
            pieces[mask] = swap(arrived, ("group", "tenant"), plane, mask)
        return pieces

    def paired(pieces):
        pieces = dict(pieces)
        for mask in range(0, plane, 2):
            pieces[mask | 1] = swap(pieces[mask], "tenant", n_owner, 1)
        return pieces

    plan = stages(n)
    firsts = [part_for(pairs) for pairs in rounds(plan[0])]
    asked = [resp_tenant] + [swap(resp_tenant, "tenant", n_owner, m) for m in range(1, n_owner)]
    pad = ((0, 0), (0, 0), (0, 1), (0, head_cols - rank))
    out_rows = jnp.concatenate([delta_out, jnp.pad(delta_scale[:, None, None, :], pad)], axis=1)
    arrived = {
        0: sum(lax.ppermute(part, "mp", pairs) for part, pairs in zip(firsts, rounds(plan[0])))
    }
    arrived[0], *asked = lax.optimization_barrier((arrived[0], *asked))
    packed_in, packed_out, pick = pack(
        me_owner.astype(I32).reshape(1), owner_map, asked, delta_in, out_rows
    )
    even = {0: crossed(arrived[0])}
    arrived[1] = arrival(plan[1], arrived[0])
    own = lax.dynamic_slice_in_dim(kv_weight, me_mp * d_shard, d_shard, 0).reshape(d_shard, cols)
    base = jnp.dot(tokens, own, preferred_element_type=F32)
    kept = lax.optimization_barrier((*even[0].values(), arrived[1], packed_in, base))
    even[0], (arrived[1], packed_in, base) = dict(zip(even[0], kept)), kept[-3:]

    def gathered(packed):
        return jnp.concatenate(
            [packed] + [swap(packed, "tenant", n_owner, m) for m in range(2, n_owner, 2)], axis=0
        )

    def needed(m, t):
        return next(at for at, to in enumerate(plan) if to[m] == m + n - t)

    low, moved, ready, sent_on = {}, [], [], []
    for t in range(1, n):
        new = t - 1
        if t == 1:
            pieces = gate(paired(even[0]))
        else:
            even[new] = crossed(tied(arrived[new], *ready))
            if t == 2:
                packed_in = tied(packed_in, *even[new].values())
                packed_out = tied(packed_out, *even[new].values())
            pieces = gate(paired(gate(even[new], *sent_on)))
        ready = [*pieces.values()]
        if t + 1 < len(plan):
            arrived[t + 1] = arrival(plan[t + 1], arrived[t])
        right = {m: needed(m, t) for m in range(t)}
        left = {n - 1 - m: at for m, at in right.items()}
        uses = [{**right, **left}] if 2 * t <= n else [right, left]
        others = {at for use in uses for at in use.values()} - {new}
        again = any(needed(m, later) == new for later in range(t + 1, n) for m in range(later))
        fused = t == 1 or (len(others) <= 1 and not again)

        def holds(use, at):
            hits = [me_mp == m for m, value in use.items() if value == at]
            return functools.reduce(jnp.logical_or, hits, jnp.zeros((), bool))

        earlier = [low[at] for at in others] if fused else []
        flags = [holds(use, *others) if earlier else jnp.zeros((), bool) for use in uses]
        spot = jnp.stack([me_share.astype(I32)] + [flag.astype(I32) for flag in flags])
        if fused:
            sent_on = step(
                tied(spot, *moved), tokens, pieces, moved, earlier, len(uses), hop_type,
                SMALL if new else LARGE,
            )
            low[new] = sent_on[0]
        else:
            low[new] = step(spot, tokens, pieces, [], [], 1, hop_type, SMALL)[0]
            sent_on = []
            for use, other in zip(uses, moved):
                value = low[new]
                for at in set(use.values()) - {new}:
                    value = jnp.where(holds(use, at), low[at], value)
                sent_on.append(value + other)
        rights = [(m, m + 1) for m in range(t)]
        lefts = [(n - 1 - m, n - 2 - m) for m in range(t)]
        if 2 * t < n:
            moved = [lax.ppermute(sent_on[0], "mp", rights + lefts)]
        else:
            moved = [lax.ppermute(sent_on[0], "mp", rights), lax.ppermute(sent_on[-1], "mp", lefts)]
    came = moved
    factors, outs = gathered(packed_in), gathered(packed_out)
    part_coeff = coefficients(
        pick, tokens, factors, swap(factors, "tenant", n_owner, 1), resp_len
    )
    part_coeff = tied(part_coeff, low[min(1, n - 2)])
    if n <= 4:
        sent_coeff = part_coeff.astype(hop_type)
        coeff = part_coeff
        for k in range(n - 1, 0, -1):
            coeff = coeff + swap(sent_coeff, "mp", n, k).astype(F32)
    else:
        coeff, mask = part_coeff, 1
        while mask < n:
            coeff = coeff + swap(coeff, "mp", n, mask)
            mask *= 2
    outs, later_pick = lax.optimization_barrier((outs, pick, part_coeff))[:2]
    all_out = jnp.concatenate((outs, swap(outs, "tenant", n_owner, 1)), axis=0)
    chosen = jnp.stack(
        [lax.dynamic_index_in_dim(all_out, later_pick[r], 0, keepdims=False) for r in range(resp_dev)]
    )
    scale = chosen[:, rank, 0, :rank].astype(F32)
    lowrank = (coeff * scale[:, :, None]).astype(BF16)
    delta = jnp.einsum(
        "rkl,rkc->rlc",
        lowrank,
        chosen[:, :rank].reshape(resp_dev, rank, cols),
        preferred_element_type=F32,
    ).reshape(tok_dev, cols)

    total = base + delta
    for value in came:
        total = total + value.astype(F32)
    return total.astype(BF16).reshape(tok_dev, 2, head_cols)


def solution(mesh):
    return jax.shard_map(
        shards,
        mesh=mesh,
        in_specs=(
            P(("group", "tenant"), "mp"),
            P(None, None, "mp"),
            P(("group", "tenant"), None, "mp"),
            P(("group", "tenant"), None, None, "mp"),
            P(("group", "tenant"), None),
            P("group"),
            P(("group", "tenant")),
        ),
        out_specs=P(("group", "tenant"), None, "mp"),
        check_vma=False,
    )
```

```python
import functools

import jax
import jax.numpy as jnp
from jax import lax
from jax.experimental import pallas as pl
from jax.experimental.pallas import tpu as pltpu
from jax.sharding import PartitionSpec as P

CAPO = 2
F32 = jnp.float32
BF16 = jnp.bfloat16
I32 = jnp.int32
VMEM_LIMIT = 20 * 1024 * 1024
SMALL = pl.CostEstimate(flops=1, bytes_accessed=1, transcendentals=0)
LARGE = pl.CostEstimate(flops=20_000_000_000, bytes_accessed=1, transcendentals=0)


def swap(value, axis, size, mask):
    return lax.ppermute(value, axis, [(i, i ^ mask) for i in range(size)])


def hop(value, n, at):
    return lax.ppermute(value, "mp", [(at, at + 1), (n - 1 - at, n - 2 - at)])


def stages(n):
    if n == 4:
        return [(3, 0, 3, 0), (2, 3, 0, 1), (1, 2, 1, 2)]
    return [tuple(m ^ k for m in range(n)) for k in range(n - 1, 0, -1)]


def rounds(targets):
    left, out = [(source, m) for m, source in enumerate(targets)], []
    while left:
        now, rest = {}, []
        for source, m in left:
            if source in now or (len(targets) == 4 and (source ^ m) != (left[0][0] ^ left[0][1])):
                rest.append((source, m))
            else:
                now[source] = m
        out.append(list(now.items()))
        left = rest
    return out


def tied(value, *others):
    return lax.optimization_barrier((value, *others))[0]


def gate(values, *others):
    kept = lax.optimization_barrier((*values.values(), *others))
    return dict(zip(values, kept))


def step_kernel(masks, arrivals, earlier, place_ref, tok_ref, *refs):
    count = len(masks)
    pieces, refs = refs[:count], refs[count:]
    extra, refs = refs[: arrivals + earlier], refs[arrivals + earlier :]
    *out_refs, weight, token, total, held, sems, held_sems = refs
    rows = weight.shape[1]
    copies = []
    for at, mask in enumerate(masks):
        here = pl.ds(pl.multiple_of((place_ref[0] ^ mask) * rows, rows), rows)
        copies.append(
            (
                pltpu.make_async_copy(pieces[at], weight.at[at], sems.at[0, at]),
                pltpu.make_async_copy(tok_ref.at[:, here], token.at[at], sems.at[1, at]),
            )
        )
    late = [
        pltpu.make_async_copy(ref, held.at[at], held_sems.at[at]) for at, ref in enumerate(extra)
    ]
    for pair in copies:
        for copy in pair:
            copy.start()
    for copy in late:
        copy.start()
    for at, pair in enumerate(copies):
        for copy in pair:
            copy.wait()
        product = jnp.dot(token[at], weight[at], preferred_element_type=F32)
        if at:
            product = total[...] + product
        if at < count - 1 or late:
            total[...] = product
        else:
            out_refs[0][...] = product.astype(out_refs[0].dtype)
    for copy in late:
        copy.wait()
    if late:
        finish(arrivals, earlier, place_ref, total, held, out_refs)


def finish(arrivals, earlier, place_ref, total, held, out_refs):
    for at, ref in enumerate(out_refs):

        def put(mine, ref=ref, at=at):
            ref[...] = (mine[...].astype(F32) + held[at].astype(F32)).astype(ref.dtype)

        if earlier:
            pl.when(place_ref[1 + at] == 1)(lambda put=put: put(held.at[arrivals]))
            pl.when(place_ref[1 + at] != 1)(lambda put=put: put(total))
        else:
            put(total)


def thin_kernel(masks, arrivals, earlier, place_ref, tok_ref, *refs):
    pieces, refs = refs[: len(masks)], refs[len(masks) :]
    extra, refs = refs[: arrivals + earlier], refs[arrivals + earlier :]
    *out_refs, weight, total, held, held_sems = refs
    rows = pieces[0].shape[0]
    late = [
        pltpu.make_async_copy(ref, held.at[at], held_sems.at[at]) for at, ref in enumerate(extra)
    ]
    for copy in late:
        copy.start()
    for mask, piece in zip(masks, pieces):
        to = pl.multiple_of((place_ref[0] ^ mask) * rows, rows)
        weight[pl.ds(to, rows), :] = piece[...]
    total[...] = jnp.dot(tok_ref[...], weight[...], preferred_element_type=F32)
    for copy in late:
        copy.wait()
    if late:
        finish(arrivals, earlier, place_ref, total, held, out_refs)
    else:
        out_refs[0][...] = total[...].astype(out_refs[0].dtype)


def step(place, tokens, pieces, arrivals, earlier, outs, out_type, cost, room=VMEM_LIMIT):
    tok_dev, depth = tokens.shape
    masks, pieces = tuple(pieces), tuple(pieces.values())
    rows, cols = pieces[0].shape
    count = len(pieces)
    extra = len(arrivals) + len(earlier)
    vmem = pl.BlockSpec(memory_space=pltpu.VMEM)
    far = pl.BlockSpec(memory_space=pl.ANY)
    held = [pltpu.VMEM((max(extra, 1), tok_dev, cols), out_type)]
    total = [pltpu.VMEM((tok_dev, cols), F32)]
    held_sems = [pltpu.SemaphoreType.DMA((max(extra, 1),))]
    if rows % 128:
        kernel, where = thin_kernel, vmem
        scratch = [pltpu.VMEM((depth, cols), BF16)] + total + held + held_sems
    else:
        kernel, where = step_kernel, far
        scratch = [
            pltpu.VMEM((count, rows, cols), BF16),
            pltpu.VMEM((count, tok_dev, rows), BF16),
        ]
        scratch += total + held + [pltpu.SemaphoreType.DMA((2, count))] + held_sems
    return pl.pallas_call(
        functools.partial(kernel, masks, len(arrivals), len(earlier)),
        out_shape=[jax.ShapeDtypeStruct((tok_dev, cols), out_type)] * outs,
        in_specs=[pl.BlockSpec(memory_space=pltpu.SMEM)] + [where] * (1 + count) + [far] * extra,
        out_specs=[vmem] * outs,
        scratch_shapes=scratch,
        compiler_params=pltpu.CompilerParams(vmem_limit_bytes=room),
        cost_estimate=cost,
        name="walk_step",
    )(place, tokens, *pieces, *arrivals, *earlier)


def pack_kernel(n_owner, ten_dev, resp_dev, owner_ref, map_ref, *refs):
    asked_refs = refs[:n_owner]
    in_ref, out_ref, in_to, out_to, pick_ref, sems = refs[n_owner:]
    me = owner_ref[0]
    asked = [map_ref[ref[r]] for ref in asked_refs for r in range(resp_dev)]

    def is_asked(slot):
        hits = [slot == other for other in asked]
        return functools.reduce(jnp.logical_or, hits).astype(I32)

    found = I32(0)
    first, second = I32(0), I32(0)
    for j in range(ten_dev):
        hit = is_asked(me * ten_dev + j)
        first = jnp.where((hit == 1) & (found == 0), j, first)
        second = jnp.where((hit == 1) & (found == 1), j, second)
        found = found + hit
    copies = []
    for c, at in enumerate((first, second)):
        copies.append(pltpu.make_async_copy(in_ref.at[at], in_to.at[c], sems.at[2 * c]))
        copies.append(pltpu.make_async_copy(out_ref.at[at], out_to.at[c], sems.at[2 * c + 1]))
    for copy in copies:
        copy.start()
    for r in range(resp_dev):
        slot = asked[r]
        owner = lax.div(slot, I32(ten_dev))
        before = I32(0)
        for j in range(ten_dev):
            other = owner * ten_dev + j
            before = before + jnp.where(other < slot, is_asked(other), 0)
        mask = owner ^ me
        pick_ref[r] = ((mask >> 1) + (mask & 1) * (n_owner // 2)) * CAPO + before
    for copy in copies:
        copy.wait()


def pack(owner, owner_map, asked, delta_in, out_rows):
    ten_dev = delta_in.shape[0]
    smem = pl.BlockSpec(memory_space=pltpu.SMEM)
    hbm = pl.BlockSpec(memory_space=pl.ANY)
    vmem = pl.BlockSpec(memory_space=pltpu.VMEM)
    return pl.pallas_call(
        functools.partial(pack_kernel, len(asked), ten_dev, asked[0].shape[0]),
        out_shape=(
            jax.ShapeDtypeStruct((CAPO,) + delta_in.shape[1:], BF16),
            jax.ShapeDtypeStruct((CAPO,) + out_rows.shape[1:], BF16),
            jax.ShapeDtypeStruct(asked[0].shape, I32),
        ),
        in_specs=[smem] * (2 + len(asked)) + [hbm, hbm],
        out_specs=(vmem, vmem, smem),
        scratch_shapes=[pltpu.SemaphoreType.DMA((2 * CAPO,))],
        compiler_params=pltpu.CompilerParams(vmem_limit_bytes=VMEM_LIMIT),
        cost_estimate=LARGE,
        name="pack_named",
    )(owner, owner_map, *asked, delta_in, out_rows)


def choose_kernel(pick_ref, mine_ref, other_ref, out_ref, sems):
    half = mine_ref.shape[0]
    for r in range(out_ref.shape[0]):
        at = pick_ref[r]

        @pl.when(at < half)
        def _(r=r, at=at):
            copy = pltpu.make_async_copy(mine_ref.at[at], out_ref.at[r], sems.at[r])
            copy.start()
            copy.wait()

        @pl.when(at >= half)
        def _(r=r, at=at):
            copy = pltpu.make_async_copy(other_ref.at[at - half], out_ref.at[r], sems.at[r])
            copy.start()
            copy.wait()


def choose(pick, mine, other):
    far = pl.BlockSpec(memory_space=pl.ANY)
    return pl.pallas_call(
        choose_kernel,
        out_shape=jax.ShapeDtypeStruct(pick.shape + mine.shape[1:], mine.dtype),
        in_specs=[pl.BlockSpec(memory_space=pltpu.SMEM), far, far],
        out_specs=pl.BlockSpec(memory_space=pltpu.VMEM),
        scratch_shapes=[pltpu.SemaphoreType.DMA(pick.shape)],
        cost_estimate=SMALL,
        name="choose_factors",
    )(pick, mine, other)


def coeff_kernel(pick_ref, tok_ref, mine_ref, other_ref, coeff_ref, *, half):
    here = pick_ref[pl.program_id(0)] < half
    factor = jnp.where(here, mine_ref[...].astype(F32), other_ref[...].astype(F32)).astype(BF16)
    coeff_ref[...] = lax.dot_general(
        factor, tok_ref[...], (((1,), (1,)), ((), ())), preferred_element_type=F32
    )


def coefficients(pick, tokens, mine, other, resp_len):
    depth = tokens.shape[1]
    half, rank = mine.shape[0], mine.shape[1]
    resp_dev = pick.shape[0]
    return pl.pallas_call(
        functools.partial(coeff_kernel, half=half),
        out_shape=jax.ShapeDtypeStruct((resp_dev, rank, resp_len), F32),
        grid_spec=pltpu.PrefetchScalarGridSpec(
            num_scalar_prefetch=1,
            grid=(resp_dev,),
            in_specs=[
                pl.BlockSpec((resp_len, depth), lambda r, p: (r, 0)),
                pl.BlockSpec((None, rank, depth), lambda r, p: (jnp.minimum(p[r], half - 1), 0, 0)),
                pl.BlockSpec((None, rank, depth), lambda r, p: (jnp.maximum(p[r] - half, 0), 0, 0)),
            ],
            out_specs=pl.BlockSpec((None, rank, resp_len), lambda r, p: (r, 0, 0)),
        ),
        compiler_params=pltpu.CompilerParams(vmem_limit_bytes=VMEM_LIMIT),
        cost_estimate=SMALL,
        name="coefficients",
    )(pick, tokens, mine, other)


def shards(tokens, kv_weight, delta_in, delta_out, delta_scale, owner_map, resp_tenant):
    tok_dev, d_shard = tokens.shape
    resp_dev = resp_tenant.shape[0]
    resp_len = tok_dev // resp_dev
    rank = delta_in.shape[1]
    head_cols = kv_weight.shape[2]
    cols = 2 * head_cols
    n_owner = lax.axis_size("tenant")
    n = lax.axis_size("mp")
    plane = lax.axis_size("group") * n_owner
    share_rows = d_shard // plane
    me_mp = lax.axis_index("mp")
    me_owner = lax.axis_index("tenant")
    me_share = lax.axis_index("group") * n_owner + me_owner
    share = me_share.astype(I32).reshape(1)
    hop_type = BF16 if n <= 4 else F32

    def part_for(pairs):
        to = sum(jnp.where(me_mp == source, target, 0) for source, target in pairs)
        row = to * d_shard + me_share * share_rows
        return lax.dynamic_slice_in_dim(kv_weight, row, share_rows, 0).reshape(share_rows, cols)

    def arrival(targets, *waits):
        return sum(
            lax.ppermute(tied(part_for(pairs), *waits), "mp", pairs) for pairs in rounds(targets)
        )

    def crossed(arrived):
        pieces = {0: arrived}
        for mask in range(2, plane, 2):
            pieces[mask] = swap(arrived, ("group", "tenant"), plane, mask)
        return pieces

    def paired(pieces):
        pieces = dict(pieces)
        for mask in range(0, plane, 2):
            pieces[mask | 1] = swap(pieces[mask], "tenant", n_owner, 1)
        return pieces

    plan = stages(n)
    firsts = [part_for(pairs) for pairs in rounds(plan[0])]
    asked = [resp_tenant] + [swap(resp_tenant, "tenant", n_owner, m) for m in range(1, n_owner)]
    pad = ((0, 0), (0, 0), (0, 1), (0, head_cols - rank))
    out_rows = jnp.concatenate([delta_out, jnp.pad(delta_scale[:, None, None, :], pad)], axis=1)
    arrived = {
        0: sum(lax.ppermute(part, "mp", pairs) for part, pairs in zip(firsts, rounds(plan[0])))
    }
    arrived[0], *asked = lax.optimization_barrier((arrived[0], *asked))
    packed_in, packed_out, pick = pack(
        me_owner.astype(I32).reshape(1), owner_map, asked, delta_in, out_rows
    )
    even = {0: crossed(arrived[0])}
    arrived[1] = arrival(plan[1], arrived[0])
    own = lax.dynamic_slice_in_dim(kv_weight, me_mp * d_shard, d_shard, 0).reshape(d_shard, cols)
    base = jnp.dot(tokens, own, preferred_element_type=F32)
    kept = lax.optimization_barrier((*even[0].values(), arrived[1], packed_in, base))
    even[0], (arrived[1], packed_in, base) = dict(zip(even[0], kept)), kept[-3:]

    def gathered(packed):
        return jnp.concatenate(
            [packed] + [swap(packed, "tenant", n_owner, m) for m in range(2, n_owner, 2)], axis=0
        )

    def needed(m, t):
        return next(at for at, to in enumerate(plan) if to[m] == m + n - t)

    low, moved, ready, sent_on = {}, [], [], []
    for t in range(1, n):
        new = t - 1
        if t == 1:
            pieces = gate(paired(even[0]))
        else:
            even[new] = crossed(tied(arrived[new], *ready))
            if t == 2:
                packed_in = tied(packed_in, *even[new].values())
                packed_out = tied(packed_out, *even[new].values())
            pieces = gate(paired(gate(even[new], *sent_on)))
        ready = [*pieces.values()]
        if t + 1 < len(plan):
            arrived[t + 1] = arrival(plan[t + 1], arrived[t])
        right = {m: needed(m, t) for m in range(t)}
        left = {n - 1 - m: at for m, at in right.items()}
        uses = [{**right, **left}] if 2 * t <= n else [right, left]
        others = {at for use in uses for at in use.values()} - {new}
        again = any(needed(m, later) == new for later in range(t + 1, n) for m in range(later))
        fused = t == 1 or (len(others) <= 1 and not again)

        def holds(use, at):
            hits = [me_mp == m for m, value in use.items() if value == at]
            return functools.reduce(jnp.logical_or, hits, jnp.zeros((), bool))

        earlier = [low[at] for at in others] if fused else []
        flags = [holds(use, *others) if earlier else jnp.zeros((), bool) for use in uses]
        spot = jnp.stack([me_share.astype(I32)] + [flag.astype(I32) for flag in flags])
        if fused:
            sent_on = step(
                tied(spot, *moved), tokens, pieces, moved, earlier, len(uses), hop_type,
                SMALL if new else LARGE, VMEM_LIMIT if t < n - 1 else 3 * VMEM_LIMIT,
            )
            low[new] = sent_on[0]
        else:
            low[new] = step(spot, tokens, pieces, [], [], 1, hop_type, SMALL)[0]
            sent_on = []
            for use, other in zip(uses, moved):
                value = low[new]
                for at in set(use.values()) - {new}:
                    value = jnp.where(holds(use, at), low[at], value)
                sent_on.append(value + other)
        rights = [(m, m + 1) for m in range(t)]
        lefts = [(n - 1 - m, n - 2 - m) for m in range(t)]
        if 2 * t < n:
            moved = [lax.ppermute(sent_on[0], "mp", rights + lefts)]
        else:
            moved = [lax.ppermute(sent_on[0], "mp", rights), lax.ppermute(sent_on[-1], "mp", lefts)]
    came = moved
    factors = gathered(packed_in)
    part_coeff = coefficients(
        pick, tokens, factors, swap(factors, "tenant", n_owner, 1), resp_len
    )
    part_coeff = tied(part_coeff, low[min(1, n - 2)])
    coeff, mask = part_coeff, 1
    while mask < n:
        kind = hop_type
        coeff = coeff + swap(coeff.astype(kind), "mp", n, mask).astype(F32)
        mask *= 2
    outs = gathered(tied(packed_out, part_coeff))
    chosen = choose(pick, outs, swap(outs, "tenant", n_owner, 1))
    scale = chosen[:, rank, 0, :rank].astype(F32)
    lowrank = (coeff * scale[:, :, None]).astype(BF16)
    delta = jnp.einsum(
        "rkl,rkc->rlc",
        lowrank,
        chosen[:, :rank].reshape(resp_dev, rank, cols),
        preferred_element_type=F32,
    ).reshape(tok_dev, cols)

    total = base + delta
    for value in came:
        total = total + value.astype(F32)
    return total.astype(BF16).reshape(tok_dev, 2, head_cols)


def solution(mesh):
    return jax.shard_map(
        shards,
        mesh=mesh,
        in_specs=(
            P(("group", "tenant"), "mp"),
            P(None, None, "mp"),
            P(("group", "tenant"), None, "mp"),
            P(("group", "tenant"), None, None, "mp"),
            P(("group", "tenant"), None),
            P("group"),
            P(("group", "tenant")),
        ),
        out_specs=P(("group", "tenant"), None, "mp"),
        check_vma=False,
    )
```
